1024 devices in a mesh: row: 64 (over z_lo, x, core), col: 16 (over y, z_hi).
Axes of the slice: x: 4, y: 4, z: 32 (z_hi: 4, z_lo: 8; z = z_hi * 8 + z_lo), core: 2. Of those that a mesh axis runs over, the one named last changes fastest.
Arguments:
- left_blocks: bfloat16 [192, 2048, 128], P('row', 'col'), may hold values from -4 to 4
- left_index: int32 [192, 32], P('row', 'col'), may hold values from -1 to 1151, as said below
- right_blocks: bfloat16 [128, 2048, 128], P('row', 'col'), may hold values from -4 to 4
- right_index: int32 [128, 32], P('row', 'col'), may hold values from 0 to 1152, as said below
- out_pattern: int32 [128, 128], P('row', 'col'), may hold values 0 or 1
Outputs:
- product: bfloat16 [16384, 16384], P('row', 'col')
The draws below stay inside these ranges and needn't reach their ends.
Inputs may be any that keep to these rules, and one draw needn't show every extreme that they name: `left_index`: column 0 of a left slot is a block row from 0 to 1; column 1 is a block column within the 72 columns of the device's grid column, or -1 for an empty slot. No two live slots of one grid row name the same pair. The live slots of a device come first, and some device has all 3 slots live. All block indices named by live slots of either pattern lie in one common set holding 2 of every 18 consecutive block indices. `right_index`: column 0 of a right slot is a block row within the 18 rows of the device's grid row, or 1152 for an empty slot; column 1 is a block column from 0 to 7. No two live slots of one device name the same pair. The live slots of a device come first, and some device has all 2 slots live.
All inputs are finite; a program needn't handle non-finite values. No bound on the sum of `out_pattern` on one device may be relied on, other than what follows from the above.
Results may differ from the reference program's by a relative error of at most 0.001.
Values may be sent and summed in bfloat16 or wider, within the bound.
No kernel may reach another device: no remote copies, remote signals or barrier semaphores. Data moves between devices by JAX's collectives and lax.ppermute only.
A program may use at most 32 MiB of HBM per device.

```python
import math
import jax
import jax.numpy as jnp
from jax import lax

BLK = 128
NBLK = 1152
BAND = 2
SLAB = 8
ACAP = 3
BCAP = 2
KROW = 18
N_ROW = 64
N_COL = 16


def common_set(key):
    group_keys = jax.random.split(key, N_ROW)
    offsets = jax.vmap(lambda k: jax.random.permutation(k, KROW)[:2])(group_keys).astype(jnp.int32)
    return jnp.arange(N_ROW, dtype=jnp.int32)[:, None] * KROW + offsets


def live_counts(key, capacity):
    first, second = jax.random.split(key)
    devices = N_ROW * N_COL
    counts = jax.random.randint(first, (devices,), 1, capacity + 1).astype(jnp.int32)
    fullest = jax.random.randint(second, (), 0, devices)
    return jnp.where(jnp.arange(devices, dtype=jnp.int32) == fullest, capacity, counts)


def draw_left_index(key, part):
    chosen = common_set(key)
    key = jax.random.fold_in(key, 11)
    ratio = N_ROW // N_COL
    width = 2 * ratio
    candidates = chosen.reshape(N_COL, width)
    devices = N_ROW * N_COL
    device_keys = jax.random.split(key, devices + 1)
    picks = jax.vmap(lambda k: jax.random.permutation(k, BAND * width)[:ACAP])(device_keys[1:]).astype(jnp.int32)
    counts = live_counts(device_keys[0], ACAP)
    column_of = jnp.arange(devices, dtype=jnp.int32) % N_COL
    band_part = picks // width
    block_part = candidates[column_of[:, None], picks % width]
    live = jnp.arange(ACAP, dtype=jnp.int32)[None, :] < counts[:, None]
    block_part = jnp.where(live, block_part, -1)
    index = jnp.stack([band_part, block_part], axis=-1)
    return index.reshape(N_ROW, N_COL, ACAP, 2).transpose(0, 2, 1, 3).reshape(N_ROW * ACAP, N_COL * 2).astype(jnp.int32)


def draw_right_index(key, part):
    chosen = common_set(key)
    key = jax.random.fold_in(key, 23)
    devices = N_ROW * N_COL
    device_keys = jax.random.split(key, devices + 1)
    picks = jax.vmap(lambda k: jax.random.permutation(k, 2 * SLAB)[:BCAP])(device_keys[1:]).astype(jnp.int32)
    counts = live_counts(device_keys[0], BCAP)
    row_of = jnp.arange(devices, dtype=jnp.int32) // N_COL
    block_part = chosen[row_of[:, None], picks % 2]
    slab_part = picks // 2
    live = jnp.arange(BCAP, dtype=jnp.int32)[None, :] < counts[:, None]
    block_part = jnp.where(live, block_part, NBLK)
    index = jnp.stack([block_part, slab_part], axis=-1)
    return index.reshape(N_ROW, N_COL, BCAP, 2).transpose(0, 2, 1, 3).reshape(N_ROW * BCAP, N_COL * 2).astype(jnp.int32)


def set_ends(entries, rng, low, high):
    longest = entries.shape.index(max(entries.shape))
    spots = []
    for shift in (0, 1):
        where = [jax.random.randint(jax.random.fold_in(rng, axis), (), 0, length) for axis, length in enumerate(entries.shape)]
        where[longest] = (where[longest] + shift) % entries.shape[longest]
        spots.append(tuple(where))
    return entries.at[spots[0]].set(low).at[spots[1]].set(high)


def shard_levels(key, shape, shards, smallest, largest):
    def one(position, shards_of):
        heights = jax.random.uniform(jax.random.fold_in(jax.random.fold_in(key, 6), position), (shards_of,), jnp.float32, smallest / len(shards), largest / len(shards))
        return jnp.repeat(jnp.exp(heights), shape[position] // shards_of).reshape((-1,) + (1,) * (len(shape) - position - 1))

    level = one(*shards[0])
    for cut in shards[1:]:
        level = level * one(*cut)
    return level


def scatter_about(key, shape, spread, most, shards=(), held_as=jnp.bfloat16):
    drawn = jax.random.normal(key, shape, jnp.float32) * spread
    if len(shards) > 0:
        drawn = shard_levels(key, shape, shards, -0.22, 0.18) * drawn
    return jnp.clip(drawn, min=-most, max=most).astype(held_as)


def setup_inputs(seed: int = 0) -> dict:
    key_list = jax.random.split(jax.random.key(seed), 6)
    left_blocks = scatter_about(key_list[0], (N_ROW * ACAP, N_COL * BLK, BLK), (BLK ** -0.25), 4.0, ((0, 64), (1, 16)))
    left_index = draw_left_index(jax.random.fold_in(key_list[5], 71), 0)
    right_blocks = scatter_about(key_list[2], (N_ROW * BCAP, N_COL * BLK, BLK), (BLK ** -0.25), 4.0, ((0, 64), (1, 16)))
    right_index = draw_right_index(jax.random.fold_in(key_list[5], 71), 0)
    out_pattern = set_ends((jax.random.randint(key_list[4], (N_ROW * BAND, N_COL * SLAB), 0, 4) < 3).astype(jnp.int32), jax.random.fold_in(key_list[4], 1), 0, 1)
    return {"left_blocks": left_blocks, "left_index": left_index, "right_blocks": right_blocks, "right_index": right_index, "out_pattern": out_pattern}


def contribute(left_all, left_keys, right_all, right_keys):
    count = right_all.shape[0]
    group = math.gcd(count, 32)
    band_rows = jnp.arange(BAND, dtype=jnp.int32)
    slot_ids = jnp.arange(left_all.shape[0], dtype=jnp.int32)
    columns = jnp.arange(SLAB, dtype=jnp.int32)
    blocks_grouped = right_all.reshape(count // group, group, BLK, BLK)
    keys_grouped = right_keys.reshape(count // group, group, 2)

    def step(total, pair):
        blocks, keys = pair
        match = (left_keys[None, None, :, 1] == keys[:, None, None, 0]) & (left_keys[None, None, :, 0] == band_rows[None, :, None])
        found = jnp.any(match, axis=2)
        where = jnp.sum(jnp.where(match, slot_ids[None, None, :], 0), axis=2).astype(jnp.int32)
        picked = jnp.where(found[:, :, None, None], left_all[where], jnp.zeros((), left_all.dtype))
        partial_value = jnp.einsum("bixy,byz->bixz", picked.astype(jnp.float32), blocks.astype(jnp.float32))
        select = (keys[:, 1:2] == columns[None, :]).astype(jnp.float32)
        return total + jnp.einsum("bj,bixz->ixjz", select, partial_value, precision=lax.Precision.HIGHEST), None

    start = jnp.zeros((BAND, BLK, SLAB, BLK), jnp.float32)
    total, unused = lax.scan(step, start, (blocks_grouped, keys_grouped))
    return total


def reference(left_blocks, left_index, right_blocks, right_index, out_pattern):
    left_grid = left_blocks.reshape(N_ROW, ACAP, N_COL, BLK, BLK).transpose(0, 2, 1, 3, 4).reshape(N_ROW, N_COL * ACAP, BLK, BLK)
    left_keys = left_index.reshape(N_ROW, ACAP, N_COL, 2).transpose(0, 2, 1, 3).reshape(N_ROW, N_COL * ACAP, 2)
    right_grid = right_blocks.reshape(N_ROW * BCAP, N_COL, BLK, BLK).transpose(1, 0, 2, 3)
    right_keys = right_index.reshape(N_ROW * BCAP, N_COL, 2).transpose(1, 0, 2)
    pattern = out_pattern.reshape(N_ROW, BAND, N_COL, SLAB).transpose(0, 2, 1, 3)

    def per_row(row_args):
        blocks, keys, masks = row_args

        def per_col(col_args):
            other_blocks, other_keys, mask = col_args
            total = contribute(blocks, keys, other_blocks, other_keys)
            kept = jnp.where(mask[:, None, :, None] > 0, total, jnp.zeros((), total.dtype))
            return kept.reshape(BAND * BLK, SLAB * BLK).astype(jnp.bfloat16)

        return lax.map(per_col, (right_grid, right_keys, masks))

    tiles = lax.map(per_row, (left_grid, left_keys, pattern))
    return tiles.transpose(0, 2, 1, 3).reshape(N_ROW * BAND * BLK, N_COL * SLAB * BLK)
```

```python
import jax
import jax.numpy as jnp
from jax import lax
from jax.experimental import pallas as pl
from jax.experimental.pallas import tpu as pltpu
from jax.sharding import PartitionSpec as P

Z_LO, X, CORE, Y, Z_HI = 8, 4, 2, 4, 4
BLK = 128
HOLD = 10**11
META = 16
A_SLOTS, B_SLOTS = 3, 2
A_ROWS = A_SLOTS * BLK + META
B_ROWS = B_SLOTS * BLK + META
K_COL = 72
K_ROW = 18


def pairs(partner):
    out = []
    for zl in range(Z_LO):
        for x in range(X):
            for q in range(CORE):
                for y in range(Y):
                    for zh in range(Z_HI):
                        a, b, c, d, e = partner(zl, x, q, y, zh)
                        out.append(
                            (
                                (((zl * X + x) * CORE + q) * Y + y) * Z_HI + zh,
                                (((a * X + b) * CORE + c) * Y + d) * Z_HI + e,
                            )
                        )
    return out


def swap(value, partner):
    return lax.ppermute(value, ("row", "col"), pairs(partner))


def z_lo_swap(value, d):
    return swap(value, lambda zl, x, q, y, zh: (zl ^ d, x, q, y, zh))


def z_hi_swap(value, first, second):
    return swap(value, lambda zl, x, q, y, zh: (zl, x, q, y, zh ^ (second if q else first)))


def y_swap(value, first, second):
    return swap(value, lambda zl, x, q, y, zh: (zl, x, q, y ^ (second if q else first), zh))


def x_swap(value, first, second):
    return swap(value, lambda zl, x, q, y, zh: (zl, x ^ (second if q else first), q, y, zh))


def core_swap(value):
    return swap(value, lambda zl, x, q, y, zh: (zl, x, q ^ 1, y, zh))


def after(value, *others):
    return lax.optimization_barrier((value, *others))[0]


def hold(value, flops=HOLD):
    def kernel(in_ref, out_ref):
        out_ref[...] = in_ref[...]

    return pl.pallas_call(
        kernel,
        out_shape=jax.ShapeDtypeStruct(value.shape, value.dtype),
        cost_estimate=pl.CostEstimate(flops=flops, bytes_accessed=0, transcendentals=0),
        name="hold",
    )(value)


def meta_rows(values):
    flat = jnp.concatenate(values).astype(jnp.bfloat16)
    return jnp.pad(flat[None, :], ((0, META - 1), (0, BLK - flat.shape[0])))


def gather(left, right):
    rows = A_ROWS
    cat = jnp.concatenate
    sibling = core_swap(left)
    right = cat([right, z_lo_swap(right, 4)])
    z_one = z_hi_swap(cat([left, sibling]), 1, 3)
    right = cat([right, z_lo_swap(right, 2)])
    z_one_mine = hold(z_one[:rows])
    right = cat([right, z_lo_swap(right, 1)])
    high = right.shape[0]
    z_two = z_hi_swap(z_one_mine, 3, 1)
    swapped = core_swap(cat([right, z_one_mine, z_one[rows:]]))
    near_right, z_other = swapped[:high], swapped[high:]
    x_one = x_swap(cat([right, near_right]), 1, 3)
    mine = cat([left, z_one_mine, z_other[rows:]])
    others = cat([sibling, z_one[rows:], z_other[:rows]])
    y_one = y_swap(cat([mine, others]), 1, 3)
    x_two = x_swap(x_one[:high], 3, 1)
    z_two = hold(z_two)
    y_two = y_swap(cat([y_one[: 3 * rows], z_two]), 3, 1)
    y_last = [y_swap(z_two, 1, 3), y_swap(z_two, 2, 2)]
    swapped = core_swap(cat([x_one, y_one[3 * rows :]]))
    x_two, y_two = lax.optimization_barrier((x_two, y_two))
    x_last = core_swap(x_two)
    return (
        [mine, y_one[: 3 * rows], y_two, swapped[2 * high :], z_two] + y_last,
        [right, near_right, x_one, swapped[: 2 * high], x_two, x_last],
    )


def product_kernel(n_left, n_right, place_ref, pattern_ref, *refs):
    left_parts = refs[:n_left]
    right_parts = refs[n_left : n_left + n_right]
    out_ref = refs[n_left + n_right]
    left, right, total, left_meta, right_meta, left_keys, right_keys, work, sems, key_sems = refs[
        n_left + n_right + 1 :
    ]
    copies = []
    for parts, held in ((left_parts, left), (right_parts, right)):
        at = 0
        for part in parts:
            copy = pltpu.make_async_copy(
                part, held.at[pl.ds(at, part.shape[0])], sems.at[len(copies)]
            )
            copy.start()
            copies.append(copy)
            at += part.shape[0]
    total[...] = jnp.zeros_like(total)
    for copy in copies:
        copy.wait()
    n_a = left_meta.shape[0]
    n_b = right_meta.shape[0]
    for i in range(n_a):
        rows = left[pl.ds(i * A_ROWS + A_SLOTS * BLK, META), :].astype(jnp.float32)
        left_meta[pl.ds(i, 1), :] = rows[0:1].astype(jnp.int32)
    for i in range(n_b):
        rows = right[pl.ds(i * B_ROWS + B_SLOTS * BLK, META), :].astype(jnp.float32)
        right_meta[pl.ds(i, 1), :] = rows[0:1].astype(jnp.int32)
    left_copy = pltpu.make_async_copy(left_meta, left_keys, key_sems.at[0])
    right_copy = pltpu.make_async_copy(right_meta, right_keys, key_sems.at[1])
    left_copy.start()
    right_copy.start()
    left_copy.wait()
    right_copy.wait()

    row = place_ref[0]
    col = place_ref[1]
    zl, x, q = row // (X * CORE), (row // CORE) % X, row % CORE
    y, zh = col // Z_HI, col % Z_HI
    near, far = jnp.where(q == 0, 1, 3), jnp.where(q == 0, 3, 1)

    def shard(i, count):
        n = jnp.where(i < 9, i, i - 1)
        p, r = n % 3, n // 3
        dz = jnp.where(p == 0, 0, jnp.where((p == 1) == (r < 3), near, far))
        dy = jnp.where(r == 0, 0, jnp.where(r == 1, near, jnp.where(r == 2, 2, far)))
        opposite = (i == 9) | (i > 12)
        dz = jnp.where(opposite, 2, dz)
        dy = jnp.where(
            opposite,
            jnp.where(i == 9, far, jnp.where(i == 13, 0, jnp.where(i == 14, near, 2))),
            dy,
        )
        there = (y ^ dy) * Z_HI + (zh ^ dz)

        def slot(s, count):
            offset = left_keys[i, s]
            band = left_keys[i, A_SLOTS + s]
            live = offset >= 0
            inside = jnp.maximum(offset, 0)
            group = inside // K_ROW
            want = inside - group * K_ROW
            other = there * (K_COL // K_ROW) + group
            e = (other % CORE) ^ q
            u = ((other // CORE) % X) ^ x
            w = (other // (X * CORE)) ^ zl
            m = ((w & 1) << 2) | (w & 2) | (w >> 2)
            part = jnp.where(
                u == 0,
                e,
                jnp.where(u == 2, 6 + e, jnp.where(u == near, 2 + e, 5 - e)),
            )
            t = part * Z_LO + m
            for j in range(B_SLOTS):
                column = right_keys[t, B_SLOTS + j]
                hit = live & (right_keys[t, j] == want) & (pattern_ref[band, column] > 0)

                @pl.when(hit)
                def _():
                    work[0, count] = i * A_ROWS + s * BLK
                    work[1, count] = t * B_ROWS + j * BLK
                    work[2, count] = band * pattern_ref.shape[1] + column

                count = count + hit.astype(jnp.int32)
            return count

        for s in range(A_SLOTS):
            count = slot(s, count)
        return count

    count = lax.fori_loop(0, n_a, shard, jnp.int32(0))

    def multiply(n, carry):
        a = left[pl.ds(pl.multiple_of(work[0, n], 16), BLK), :]
        b = right[pl.ds(pl.multiple_of(work[1, n], 16), BLK), :]
        total[work[2, n]] += jnp.dot(a, b, preferred_element_type=jnp.float32)
        return carry

    lax.fori_loop(0, count, multiply, 0)
    band, slab = pattern_ref.shape
    for i in range(band):
        for j in range(slab):
            out_ref[i * BLK : (i + 1) * BLK, j * BLK : (j + 1) * BLK] = total[i * slab + j].astype(
                out_ref.dtype
            )


def multiply_parts(left_parts, right_parts, row, col, pattern):
    band, slab = pattern.shape
    n_a = sum(p.shape[0] for p in left_parts) // A_ROWS
    n_b = sum(p.shape[0] for p in right_parts) // B_ROWS
    n_parts = len(left_parts) + len(right_parts)
    smem = pl.BlockSpec(memory_space=pltpu.SMEM)
    anywhere = pl.BlockSpec(memory_space=pl.ANY)
    place = jnp.stack([row, col]).astype(jnp.int32)

    def kernel(*refs):
        product_kernel(len(left_parts), len(right_parts), *refs)

    return pl.pallas_call(
        kernel,
        out_shape=jax.ShapeDtypeStruct((band * BLK, slab * BLK), jnp.bfloat16),
        in_specs=[smem, smem] + [anywhere] * n_parts,
        out_specs=pl.BlockSpec(memory_space=pltpu.VMEM),
        scratch_shapes=[
            pltpu.VMEM((n_a * A_ROWS, BLK), jnp.bfloat16),
            pltpu.VMEM((n_b * B_ROWS, BLK), jnp.bfloat16),
            pltpu.VMEM((band * slab, BLK, BLK), jnp.float32),
            pltpu.VMEM((n_a, BLK), jnp.int32),
            pltpu.VMEM((n_b, BLK), jnp.int32),
            pltpu.SMEM((n_a, BLK), jnp.int32),
            pltpu.SMEM((n_b, BLK), jnp.int32),
            pltpu.SMEM((3, n_a * A_SLOTS * B_SLOTS), jnp.int32),
            pltpu.SemaphoreType.DMA((n_parts,)),
            pltpu.SemaphoreType.DMA((2,)),
        ],
        compiler_params=pltpu.CompilerParams(vmem_limit_bytes=24 * 1024 * 1024),
        name="block_products",
    )(place, pattern, *left_parts, *right_parts)


def per_device(left_blocks, left_index, right_blocks, right_index, out_pattern):
    row = lax.axis_index("row")
    col = lax.axis_index("col")
    offset = jnp.where(left_index[:, 1] >= 0, left_index[:, 1] - col * K_COL, -1)
    left = jnp.concatenate(
        [left_blocks.reshape(-1, BLK), meta_rows([offset, left_index[:, 0]])]
    )
    live = right_index[:, 0] < (row + 1) * K_ROW
    offset = jnp.where(live, right_index[:, 0] - row * K_ROW, -1)
    right = jnp.concatenate(
        [right_blocks.reshape(-1, BLK), meta_rows([offset, jnp.where(live, right_index[:, 1], 0)])]
    )
    return multiply_parts(*gather(left, right), row, col, out_pattern)


def solution(mesh):
    placed = (
        P("row", "col", None),
        P("row", "col"),
        P("row", "col", None),
        P("row", "col"),
        P("row", "col"),
    )
    return jax.shard_map(
        per_device, mesh=mesh, in_specs=placed, out_specs=P("row", "col"), check_vma=False
    )
```

```python
import jax
import jax.numpy as jnp
from jax import lax
from jax.experimental import pallas as pl
from jax.experimental.pallas import tpu as pltpu
from jax.sharding import PartitionSpec as P

Z_LO, X, CORE, Y, Z_HI = 8, 4, 2, 4, 4
BLK = 128
HOLD = 10**11
GROUP = 4
META = 16
A_SLOTS, B_SLOTS = 3, 2
A_ROWS = A_SLOTS * BLK + META
B_ROWS = B_SLOTS * BLK + META
K_COL = 72
K_ROW = 18


def pairs(partner):
    out = []
    for zl in range(Z_LO):
        for x in range(X):
            for q in range(CORE):
                for y in range(Y):
                    for zh in range(Z_HI):
                        a, b, c, d, e = partner(zl, x, q, y, zh)
                        out.append(
                            (
                                (((zl * X + x) * CORE + q) * Y + y) * Z_HI + zh,
                                (((a * X + b) * CORE + c) * Y + d) * Z_HI + e,
                            )
                        )
    return out


def swap(value, partner):
    return lax.ppermute(value, ("row", "col"), pairs(partner))


def z_lo_swap(value, d):
    return swap(value, lambda zl, x, q, y, zh: (zl ^ d, x, q, y, zh))


def z_hi_swap(value, first, second):
    return swap(value, lambda zl, x, q, y, zh: (zl, x, q, y, zh ^ (second if q else first)))


def y_swap(value, first, second):
    return swap(value, lambda zl, x, q, y, zh: (zl, x, q, y ^ (second if q else first), zh))


def x_swap(value, first, second):
    return swap(value, lambda zl, x, q, y, zh: (zl, x ^ (second if q else first), q, y, zh))


def core_swap(value):
    return swap(value, lambda zl, x, q, y, zh: (zl, x, q ^ 1, y, zh))


def after(value, *others):
    return lax.optimization_barrier((value, *others))[0]


def hold(value, flops):
    def kernel(in_ref, out_ref):
        out_ref[...] = in_ref[...]

    head = pl.pallas_call(
        kernel,
        out_shape=jax.ShapeDtypeStruct((META, value.shape[1]), value.dtype),
        cost_estimate=pl.CostEstimate(flops=flops, bytes_accessed=0, transcendentals=0),
        name="hold",
    )(value[:META])
    return jnp.concatenate([head, value[META:]])


def pack_kernel(left_index, right_index, left_blocks, right_blocks, left_out, right_out, sems):
    copies = []
    for blocks, out in ((left_blocks, left_out), (right_blocks, right_out)):
        for s in range(blocks.shape[0]):
            copy = pltpu.make_async_copy(
                blocks.at[s], out.at[pl.ds(s * BLK, BLK)], sems.at[len(copies)]
            )
            copy.start()
            copies.append(copy)
    lane = lax.broadcasted_iota(jnp.int32, (META, BLK), 1)

    def write(out, values):
        meta = jnp.zeros((META, BLK), jnp.int32)
        for n, value in enumerate(values):
            meta = jnp.where(lane == n, value, meta)
        out[pl.ds(out.shape[0] - META, META), :] = meta.astype(jnp.float32).astype(jnp.bfloat16)

    row, col = lax.axis_index("row"), lax.axis_index("col")
    columns = [left_index[s, 1] for s in range(A_SLOTS)]
    offsets = [jnp.where(k >= 0, k - col * K_COL, -1) for k in columns]
    bands = [jnp.clip(left_index[s, 0], 0, 1) for s in range(A_SLOTS)]
    write(left_out, offsets + bands)
    offsets = [right_index[s, 0] - row * K_ROW for s in range(B_SLOTS)]
    live = [o < K_ROW for o in offsets]
    offsets = [jnp.where(f, o, -1) for f, o in zip(live, offsets)]
    write(right_out, offsets + [jnp.where(live[s], right_index[s, 1], 0) for s in range(B_SLOTS)])
    for copy in copies:
        copy.wait()


def pack(left_index, right_index, left_blocks, right_blocks):
    smem = pl.BlockSpec(memory_space=pltpu.SMEM)
    anywhere = pl.BlockSpec(memory_space=pl.ANY)
    vmem = pl.BlockSpec(memory_space=pltpu.VMEM)
    return pl.pallas_call(
        pack_kernel,
        out_shape=[
            jax.ShapeDtypeStruct((A_ROWS, BLK), jnp.bfloat16),
            jax.ShapeDtypeStruct((B_ROWS, BLK), jnp.bfloat16),
        ],
        in_specs=[smem, smem, anywhere, anywhere],
        out_specs=[vmem, vmem],
        scratch_shapes=[pltpu.SemaphoreType.DMA((A_SLOTS + B_SLOTS,))],
        compiler_params=pltpu.CompilerParams(vmem_limit_bytes=56 * 1024 * 1024),
        name="pack",
    )(left_index, right_index, left_blocks, right_blocks)


def gather(left, right):
    rows = A_ROWS
    cat = jnp.concatenate
    sibling = core_swap(left)
    right = cat([right, z_lo_swap(right, 4)])
    z_one = z_hi_swap(cat([left, sibling]), 1, 3)
    right = cat([right, z_lo_swap(right, 2)])
    z_one_mine = hold(z_one[:rows], HOLD)
    right = cat([right, z_lo_swap(right, 1)])
    high = right.shape[0]
    z_two = z_hi_swap(z_one[:rows], 3, 1)
    swapped = core_swap(cat([right, z_one_mine, z_one[rows:]]))
    near_right, z_other = swapped[:high], swapped[high:]
    x_one = x_swap(cat([right, near_right]), 1, 3)
    mine = cat([left, z_one_mine, z_other[rows:]])
    others = cat([sibling, z_one[rows:], z_other[:rows]])
    others, z_two = lax.optimization_barrier((others, z_two))
    y_one = y_swap(cat([mine, others]), 1, 3)
    z_near = y_swap(z_two, 1, 3)
    x_one, y_one, z_near = lax.optimization_barrier((x_one, y_one, z_near))
    x_two = x_swap(x_one[:high], 3, 1)
    y_two = y_swap(cat([y_one[: 3 * rows], z_two, z_near]), 3, 1)
    swapped = core_swap(cat([x_one, y_one[3 * rows :]]))
    x_last = core_swap(x_two)
    return (
        [mine, y_one[: 3 * rows], y_two, swapped[2 * high :], z_two, z_near],
        [right, near_right, x_one, swapped[: 2 * high], x_two, x_last],
    )


def product_kernel(n_left, n_right, pattern_ref, *refs):
    left_parts = refs[:n_left]
    right_parts = refs[n_left : n_left + n_right]
    out_ref = refs[n_left + n_right]
    (
        left,
        right,
        total,
        left_raw,
        right_raw,
        left_meta,
        right_meta,
        left_keys,
        right_keys,
        work,
        sems,
        raw_sems,
        key_sems,
    ) = refs[n_left + n_right + 1 :]
    raw_copies, copies = [], []
    for parts, raw, rows in ((left_parts, left_raw, A_ROWS), (right_parts, right_raw, B_ROWS)):
        at = 0
        for part in parts:
            n = part.shape[0]
            copy = pltpu.make_async_copy(
                part.at[:, pl.ds(rows - META, META), :],
                raw.at[pl.ds(at, n)],
                raw_sems.at[len(raw_copies)],
            )
            copy.start()
            raw_copies.append(copy)
            at += n
    for parts, held in ((left_parts, left), (right_parts, right)):
        at = 0
        for part in parts:
            n = part.shape[0]
            copy = pltpu.make_async_copy(part, held.at[pl.ds(at, n)], sems.at[len(copies)])
            copy.start()
            copies.append(copy)
            at += n
    total[...] = jnp.zeros_like(total)
    for copy in raw_copies:
        copy.wait()
    n_a, n_b = left_meta.shape[0], right_meta.shape[0]
    for i in range(n_a):
        left_meta[pl.ds(i, 1), :] = left_raw[i].astype(jnp.float32)[0:1].astype(jnp.int32)
    for i in range(n_b):
        right_meta[pl.ds(i, 1), :] = right_raw[i].astype(jnp.float32)[0:1].astype(jnp.int32)
    right_copy = pltpu.make_async_copy(right_meta, right_keys, key_sems.at[1])
    right_copy.start()

    row, col = lax.axis_index("row"), lax.axis_index("col")
    zl, x, q = row // (X * CORE), (row // CORE) % X, row % CORE
    y, zh = col // Z_HI, col % Z_HI
    near, far = jnp.where(q == 0, 1, 3), jnp.where(q == 0, 3, 1)
    i = lax.broadcasted_iota(jnp.int32, left_meta.shape, 0)
    lane = lax.broadcasted_iota(jnp.int32, left_meta.shape, 1)
    first = i < 9
    n = jnp.where(first, i, i - 2)
    r = (n >= 3).astype(jnp.int32) + (n >= 6).astype(jnp.int32) + (n >= 9).astype(jnp.int32)
    p = n - 3 * r
    one = jnp.where(first, near, far)
    two = jnp.where(first, far, near)
    dz = jnp.where(p == 0, 0, jnp.where(p == 1, one, two))
    dy = jnp.where(r == 0, 0, jnp.where(r == 1, near, jnp.where(r == 2, 2, far)))
    opposite = (i == 9) | (i == 10) | (i > 13)
    dz = jnp.where(opposite, 2, dz)
    dy = jnp.where(
        opposite,
        jnp.where(i == 9, far, jnp.where(i == 10, 2, jnp.where(i == 14, 0, near))),
        dy,
    )
    there = ((y ^ dy) << 2) + (zh ^ dz)
    meta = left_meta[...]
    live = meta >= 0
    offset = jnp.maximum(meta, 0)
    group = jnp.zeros_like(offset)
    for bound in range(K_ROW, K_COL, K_ROW):
        group += (offset >= bound).astype(jnp.int32)
    want = jnp.where(live, offset - group * K_ROW, K_ROW)
    other = there * (K_COL // K_ROW) + group
    e = (other & 1) ^ q
    u = ((other >> 1) & 3) ^ x
    w = (other >> 3) ^ zl
    m = ((w & 1) << 2) | (w & 2) | (w >> 2)
    part = jnp.where(
        u == 0,
        e,
        jnp.where(u == 2, 6 + e, jnp.where(u == near, 2 + e, 5 - e)),
    )
    code = ((part * Z_LO + m) << 8) | want
    left_meta[...] = jnp.where(lane < A_SLOTS, code, meta)
    left_copy = pltpu.make_async_copy(left_meta, left_keys, key_sems.at[0])
    left_copy.start()
    right_copy.wait()
    left_copy.wait()
    slab = pattern_ref.shape[1]
    spare = pattern_ref.shape[0] * slab

    def shard(i, count):
        for s in range(A_SLOTS):
            found = left_keys[i, s]
            band = left_keys[i, A_SLOTS + s]
            t = found >> 8
            wanted = found & 255
            for j in range(B_SLOTS):
                column = right_keys[t, B_SLOTS + j]
                hit = (right_keys[t, j] == wanted) & (pattern_ref[band, column] > 0)
                work[0, count] = i * A_SLOTS + s
                work[1, count] = t * B_SLOTS + j
                work[2, count] = band * slab + column
                count = count + hit.astype(jnp.int32)
        return count

    count = lax.fori_loop(0, n_a, shard, jnp.int32(0))
    for n in range(GROUP):
        work[0, count + n] = 0
        work[1, count + n] = 0
        work[2, count + n] = spare
    for copy in copies:
        copy.wait()

    def multiply(g, carry):
        products = []
        for n in range(GROUP):
            a, b = work[0, g * GROUP + n], work[1, g * GROUP + n]
            a_shard = a // A_SLOTS
            a_at = pl.multiple_of((a - a_shard * A_SLOTS) * BLK, BLK)
            b_at = pl.multiple_of((b & 1) * BLK, BLK)
            products.append(
                jnp.dot(
                    left[a_shard, pl.ds(a_at, BLK), :],
                    right[b >> 1, pl.ds(b_at, BLK), :],
                    preferred_element_type=jnp.float32,
                )
            )
        for n in range(GROUP):
            total[work[2, g * GROUP + n]] += products[n]
        return carry

    lax.fori_loop(0, (count + GROUP - 1) // GROUP, multiply, 0)
    for b in range(pattern_ref.shape[0]):
        for j in range(slab):
            out_ref[b * BLK : (b + 1) * BLK, j * BLK : (j + 1) * BLK] = total[b * slab + j].astype(
                out_ref.dtype
            )


def multiply_parts(left_parts, right_parts, pattern):
    band, slab = pattern.shape
    left_parts = [p.reshape(-1, A_ROWS, BLK) for p in left_parts]
    right_parts = [p.reshape(-1, B_ROWS, BLK) for p in right_parts]
    n_a = sum(p.shape[0] for p in left_parts)
    n_b = sum(p.shape[0] for p in right_parts)
    n_parts = len(left_parts) + len(right_parts)
    smem = pl.BlockSpec(memory_space=pltpu.SMEM)
    anywhere = pl.BlockSpec(memory_space=pl.ANY)

    def kernel(*refs):
        product_kernel(len(left_parts), len(right_parts), *refs)

    return pl.pallas_call(
        kernel,
        out_shape=jax.ShapeDtypeStruct((band * BLK, slab * BLK), jnp.bfloat16),
        in_specs=[smem] + [anywhere] * n_parts,
        out_specs=pl.BlockSpec(memory_space=pltpu.VMEM),
        scratch_shapes=[
            pltpu.VMEM((n_a, A_ROWS, BLK), jnp.bfloat16),
            pltpu.VMEM((n_b, B_ROWS, BLK), jnp.bfloat16),
            pltpu.VMEM((band * slab + 1, BLK, BLK), jnp.float32),
            pltpu.VMEM((n_a, META, BLK), jnp.bfloat16),
            pltpu.VMEM((n_b, META, BLK), jnp.bfloat16),
            pltpu.VMEM((n_a, BLK), jnp.int32),
            pltpu.VMEM((n_b, BLK), jnp.int32),
            pltpu.SMEM((n_a, BLK), jnp.int32),
            pltpu.SMEM((n_b, BLK), jnp.int32),
            pltpu.SMEM((3, n_a * A_SLOTS * B_SLOTS + GROUP), jnp.int32),
            pltpu.SemaphoreType.DMA((n_parts,)),
            pltpu.SemaphoreType.DMA((n_parts,)),
            pltpu.SemaphoreType.DMA((2,)),
        ],
        compiler_params=pltpu.CompilerParams(vmem_limit_bytes=24 * 1024 * 1024),
        name="block_products",
    )(pattern, *left_parts, *right_parts)


def per_device(left_blocks, left_index, right_blocks, right_index, out_pattern):
    left, right = pack(left_index, right_index, left_blocks, right_blocks)
    return multiply_parts(*gather(left, right), out_pattern)


def solution(mesh):
    placed = (
        P("row", "col", None),
        P("row", "col"),
        P("row", "col", None),
        P("row", "col"),
        P("row", "col"),
    )
    return jax.shard_map(
        per_device, mesh=mesh, in_specs=placed, out_specs=P("row", "col"), check_vma=False
    )
```

```python
import jax
import jax.numpy as jnp
from jax import lax
from jax.experimental import pallas as pl
from jax.experimental.pallas import tpu as pltpu
from jax.sharding import PartitionSpec as P

Z_LO, X, CORE, Y, Z_HI = 8, 4, 2, 4, 4
BLK = 128
HOLD = 10**11
GROUP = 4
META = 16
A_SLOTS, B_SLOTS = 3, 2
A_ROWS = A_SLOTS * BLK + META
B_ROWS = B_SLOTS * BLK + META
K_COL = 72
K_ROW = 18


def pairs(partner):
    out = []
    for zl in range(Z_LO):
        for x in range(X):
            for q in range(CORE):
                for y in range(Y):
                    for zh in range(Z_HI):
                        a, b, c, d, e = partner(zl, x, q, y, zh)
                        out.append(
                            (
                                (((zl * X + x) * CORE + q) * Y + y) * Z_HI + zh,
                                (((a * X + b) * CORE + c) * Y + d) * Z_HI + e,
                            )
                        )
    return out


def swap(value, partner):
    return lax.ppermute(value, ("row", "col"), pairs(partner))


def z_lo_swap(value, d):
    return swap(value, lambda zl, x, q, y, zh: (zl ^ d, x, q, y, zh))


def z_hi_swap(value, first, second):
    return swap(value, lambda zl, x, q, y, zh: (zl, x, q, y, zh ^ (second if q else first)))


def y_swap(value, first, second):
    return swap(value, lambda zl, x, q, y, zh: (zl, x, q, y ^ (second if q else first), zh))


def x_swap(value, first, second):
    return swap(value, lambda zl, x, q, y, zh: (zl, x ^ (second if q else first), q, y, zh))


def core_swap(value):
    return swap(value, lambda zl, x, q, y, zh: (zl, x, q ^ 1, y, zh))


def after(value, *others):
    return lax.optimization_barrier((value, *others))[0]


def hold(value, flops):
    def kernel(in_ref, out_ref):
        out_ref[...] = in_ref[...]

    head = pl.pallas_call(
        kernel,
        out_shape=jax.ShapeDtypeStruct((META, value.shape[1]), value.dtype),
        cost_estimate=pl.CostEstimate(flops=flops, bytes_accessed=0, transcendentals=0),
        name="hold",
    )(value[:META])
    return jnp.concatenate([head, value[META:]])


def pack_kernel(left_index, right_index, left_blocks, right_blocks, left_out, right_out, sems):
    copies = []
    for blocks, out in ((left_blocks, left_out), (right_blocks, right_out)):
        for s in range(blocks.shape[0]):
            copy = pltpu.make_async_copy(
                blocks.at[s], out.at[pl.ds(s * BLK, BLK)], sems.at[len(copies)]
            )
            copy.start()
            copies.append(copy)
    lane = lax.broadcasted_iota(jnp.int32, (META, BLK), 1)

    def write(out, values):
        meta = jnp.zeros((META, BLK), jnp.int32)
        for n, value in enumerate(values):
            meta = jnp.where(lane == n, value, meta)
        out[pl.ds(out.shape[0] - META, META), :] = meta.astype(jnp.float32).astype(jnp.bfloat16)

    row, col = lax.axis_index("row"), lax.axis_index("col")
    columns = [left_index[s, 1] for s in range(A_SLOTS)]
    offsets = [jnp.where(k >= 0, k - col * K_COL, -1) for k in columns]
    bands = [jnp.clip(left_index[s, 0], 0, 1) for s in range(A_SLOTS)]
    write(left_out, offsets + bands)
    offsets = [right_index[s, 0] - row * K_ROW for s in range(B_SLOTS)]
    live = [o < K_ROW for o in offsets]
    offsets = [jnp.where(f, o, -1) for f, o in zip(live, offsets)]
    write(right_out, offsets + [jnp.where(live[s], right_index[s, 1], 0) for s in range(B_SLOTS)])
    for copy in copies:
        copy.wait()


def pack(left_index, right_index, left_blocks, right_blocks):
    smem = pl.BlockSpec(memory_space=pltpu.SMEM)
    anywhere = pl.BlockSpec(memory_space=pl.ANY)
    vmem = pl.BlockSpec(memory_space=pltpu.VMEM)
    return pl.pallas_call(
        pack_kernel,
        out_shape=[
            jax.ShapeDtypeStruct((A_ROWS, BLK), jnp.bfloat16),
            jax.ShapeDtypeStruct((B_ROWS, BLK), jnp.bfloat16),
        ],
        in_specs=[smem, smem, anywhere, anywhere],
        out_specs=[vmem, vmem],
        scratch_shapes=[pltpu.SemaphoreType.DMA((A_SLOTS + B_SLOTS,))],
        compiler_params=pltpu.CompilerParams(vmem_limit_bytes=56 * 1024 * 1024),
        name="pack",
    )(left_index, right_index, left_blocks, right_blocks)


def gather(left, right):
    rows = A_ROWS
    cat = jnp.concatenate
    sibling = core_swap(left)
    right = cat([right, z_lo_swap(right, 4)])
    z_one = z_hi_swap(cat([left, sibling]), 1, 3)
    right = cat([right, z_lo_swap(right, 2)])
    z_one_mine = hold(z_one[:rows], HOLD)
    right = cat([right, z_lo_swap(right, 1)])
    high = right.shape[0]
    z_two = z_hi_swap(z_one[:rows], 3, 1)
    swapped = core_swap(cat([right, z_one_mine, z_one[rows:]]))
    near_right, z_other = swapped[:high], swapped[high:]
    x_one = x_swap(cat([right, near_right]), 1, 3)
    mine = cat([left, z_one_mine, z_other[rows:]])
    others = cat([sibling, z_one[rows:], z_other[:rows]])
    others, z_two = lax.optimization_barrier((others, z_two))
    y_one = y_swap(cat([mine, others]), 1, 3)
    z_near = y_swap(z_two, 1, 3)
    y_one, z_near = lax.optimization_barrier((y_one, z_near))
    x_two = x_swap(x_one[:high], 3, 1)
    x_other = core_swap(x_one)
    y_two = y_swap(cat([y_one[: 3 * rows], z_two, z_near]), 3, 1)
    swapped = core_swap(cat([x_two, y_one[3 * rows :]]))
    return (
        [mine, y_one[: 3 * rows], y_two, swapped[high:], z_two, z_near],
        [right, near_right, x_one, x_other, x_two, swapped[:high]],
    )


def product_kernel(n_left, n_right, pattern_ref, *refs):
    left_parts = refs[:n_left]
    right_parts = refs[n_left : n_left + n_right]
    out_ref = refs[n_left + n_right]
    (
        left,
        right,
        total,
        left_raw,
        right_raw,
        left_meta,
        right_meta,
        left_keys,
        right_keys,
        work,
        sems,
        raw_sems,
        key_sems,
    ) = refs[n_left + n_right + 1 :]
    raw_copies, copies = [], []
    for parts, raw, rows in ((left_parts, left_raw, A_ROWS), (right_parts, right_raw, B_ROWS)):
        at = 0
        for part in parts:
            n = part.shape[0]
            copy = pltpu.make_async_copy(
                part.at[:, pl.ds(rows - META, META), :],
                raw.at[pl.ds(at, n)],
                raw_sems.at[len(raw_copies)],
            )
            copy.start()
            raw_copies.append(copy)
            at += n
    for parts, held in ((left_parts, left), (right_parts, right)):
        at = 0
        for part in parts:
            n = part.shape[0]
            copy = pltpu.make_async_copy(part, held.at[pl.ds(at, n)], sems.at[len(copies)])
            copy.start()
            copies.append(copy)
            at += n
    total[...] = jnp.zeros_like(total)
    for copy in raw_copies:
        copy.wait()
    n_a, n_b = left_meta.shape[0], right_meta.shape[0]
    for i in range(n_a):
        left_meta[pl.ds(i, 1), :] = left_raw[i].astype(jnp.float32)[0:1].astype(jnp.int32)
    for i in range(n_b):
        right_meta[pl.ds(i, 1), :] = right_raw[i].astype(jnp.float32)[0:1].astype(jnp.int32)
    right_copy = pltpu.make_async_copy(right_meta, right_keys, key_sems.at[1])
    right_copy.start()

    row, col = lax.axis_index("row"), lax.axis_index("col")
    zl, x, q = row // (X * CORE), (row // CORE) % X, row % CORE
    y, zh = col // Z_HI, col % Z_HI
    near, far = jnp.where(q == 0, 1, 3), jnp.where(q == 0, 3, 1)
    i = lax.broadcasted_iota(jnp.int32, left_meta.shape, 0)
    lane = lax.broadcasted_iota(jnp.int32, left_meta.shape, 1)
    first = i < 9
    n = jnp.where(first, i, i - 2)
    r = (n >= 3).astype(jnp.int32) + (n >= 6).astype(jnp.int32) + (n >= 9).astype(jnp.int32)
    p = n - 3 * r
    one = jnp.where(first, near, far)
    two = jnp.where(first, far, near)
    dz = jnp.where(p == 0, 0, jnp.where(p == 1, one, two))
    dy = jnp.where(r == 0, 0, jnp.where(r == 1, near, jnp.where(r == 2, 2, far)))
    opposite = (i == 9) | (i == 10) | (i > 13)
    dz = jnp.where(opposite, 2, dz)
    dy = jnp.where(
        opposite,
        jnp.where(i == 9, far, jnp.where(i == 10, 2, jnp.where(i == 14, 0, near))),
        dy,
    )
    there = ((y ^ dy) << 2) + (zh ^ dz)
    meta = left_meta[...]
    live = meta >= 0
    offset = jnp.maximum(meta, 0)
    group = jnp.zeros_like(offset)
    for bound in range(K_ROW, K_COL, K_ROW):
        group += (offset >= bound).astype(jnp.int32)
    want = jnp.where(live, offset - group * K_ROW, K_ROW)
    other = there * (K_COL // K_ROW) + group
    e = (other & 1) ^ q
    u = ((other >> 1) & 3) ^ x
    w = (other >> 3) ^ zl
    m = ((w & 1) << 2) | (w & 2) | (w >> 2)
    part = jnp.where(
        u == 0,
        e,
        jnp.where(u == 2, 6 + e, jnp.where(u == near, 2 + e, 5 - e)),
    )
    code = ((part * Z_LO + m) << 8) | want
    left_meta[...] = jnp.where(lane < A_SLOTS, code, meta)
    left_copy = pltpu.make_async_copy(left_meta, left_keys, key_sems.at[0])
    left_copy.start()
    right_copy.wait()
    left_copy.wait()
    slab = pattern_ref.shape[1]
    spare = pattern_ref.shape[0] * slab

    def shard(i, count):
        for s in range(A_SLOTS):
            found = left_keys[i, s]
            band = left_keys[i, A_SLOTS + s]
            t = found >> 8
            wanted = found & 255
            for j in range(B_SLOTS):
                column = right_keys[t, B_SLOTS + j]
                hit = (right_keys[t, j] == wanted) & (pattern_ref[band, column] > 0)
                work[0, count] = i * A_SLOTS + s
                work[1, count] = t * B_SLOTS + j
                work[2, count] = band * slab + column
                count = count + hit.astype(jnp.int32)
        return count

    count = lax.fori_loop(0, n_a, shard, jnp.int32(0))
    for n in range(GROUP):
        work[0, count + n] = 0
        work[1, count + n] = 0
        work[2, count + n] = spare
    for copy in copies:
        copy.wait()

    def multiply(g, carry):
        products = []
        for n in range(GROUP):
            a, b = work[0, g * GROUP + n], work[1, g * GROUP + n]
            a_shard = a // A_SLOTS
            a_at = pl.multiple_of((a - a_shard * A_SLOTS) * BLK, BLK)
            b_at = pl.multiple_of((b & 1) * BLK, BLK)
            products.append(
                jnp.dot(
                    left[a_shard, pl.ds(a_at, BLK), :],
                    right[b >> 1, pl.ds(b_at, BLK), :],
                    preferred_element_type=jnp.float32,
                )
            )
        for n in range(GROUP):
            total[work[2, g * GROUP + n]] += products[n]
        return carry

    lax.fori_loop(0, (count + GROUP - 1) // GROUP, multiply, 0)
    for b in range(pattern_ref.shape[0]):
        for j in range(slab):
            out_ref[b * BLK : (b + 1) * BLK, j * BLK : (j + 1) * BLK] = total[b * slab + j].astype(
                out_ref.dtype
            )


def multiply_parts(left_parts, right_parts, pattern):
    band, slab = pattern.shape
    left_parts = [p.reshape(-1, A_ROWS, BLK) for p in left_parts]
    right_parts = [p.reshape(-1, B_ROWS, BLK) for p in right_parts]
    n_a = sum(p.shape[0] for p in left_parts)
    n_b = sum(p.shape[0] for p in right_parts)
    n_parts = len(left_parts) + len(right_parts)
    smem = pl.BlockSpec(memory_space=pltpu.SMEM)
    anywhere = pl.BlockSpec(memory_space=pl.ANY)

    def kernel(*refs):
        product_kernel(len(left_parts), len(right_parts), *refs)

    return pl.pallas_call(
        kernel,
        out_shape=jax.ShapeDtypeStruct((band * BLK, slab * BLK), jnp.bfloat16),
        in_specs=[smem] + [anywhere] * n_parts,
        out_specs=pl.BlockSpec(memory_space=pltpu.VMEM),
        scratch_shapes=[
            pltpu.VMEM((n_a, A_ROWS, BLK), jnp.bfloat16),
            pltpu.VMEM((n_b, B_ROWS, BLK), jnp.bfloat16),
            pltpu.VMEM((band * slab + 1, BLK, BLK), jnp.float32),
            pltpu.VMEM((n_a, META, BLK), jnp.bfloat16),
            pltpu.VMEM((n_b, META, BLK), jnp.bfloat16),
            pltpu.VMEM((n_a, BLK), jnp.int32),
            pltpu.VMEM((n_b, BLK), jnp.int32),
            pltpu.SMEM((n_a, BLK), jnp.int32),
            pltpu.SMEM((n_b, BLK), jnp.int32),
            pltpu.SMEM((3, n_a * A_SLOTS * B_SLOTS + GROUP), jnp.int32),
            pltpu.SemaphoreType.DMA((n_parts,)),
            pltpu.SemaphoreType.DMA((n_parts,)),
            pltpu.SemaphoreType.DMA((2,)),
        ],
        compiler_params=pltpu.CompilerParams(vmem_limit_bytes=24 * 1024 * 1024),
        name="block_products",
    )(pattern, *left_parts, *right_parts)


def per_device(left_blocks, left_index, right_blocks, right_index, out_pattern):
    left, right = pack(left_index, right_index, left_blocks, right_blocks)
    return multiply_parts(*gather(left, right), out_pattern)


def solution(mesh):
    placed = (
        P("row", "col", None),
        P("row", "col"),
        P("row", "col", None),
        P("row", "col"),
        P("row", "col"),
    )
    return jax.shard_map(
        per_device, mesh=mesh, in_specs=placed, out_specs=P("row", "col"), check_vma=False
    )
```

```python
import jax
import jax.numpy as jnp
from jax import lax
from jax.experimental import pallas as pl
from jax.experimental.pallas import tpu as pltpu
from jax.sharding import PartitionSpec as P

Z_LO, X, CORE, Y, Z_HI = 8, 4, 2, 4, 4
BLK = 128
HOLD = 10**11
GROUP = 4
META = 16
A_SLOTS, B_SLOTS = 3, 2
A_ROWS = A_SLOTS * BLK + META
B_ROWS = B_SLOTS * BLK + META
K_COL = 72
K_ROW = 18


def pairs(partner):
    out = []
    for zl in range(Z_LO):
        for x in range(X):
            for q in range(CORE):
                for y in range(Y):
                    for zh in range(Z_HI):
                        a, b, c, d, e = partner(zl, x, q, y, zh)
                        out.append(
                            (
                                (((zl * X + x) * CORE + q) * Y + y) * Z_HI + zh,
                                (((a * X + b) * CORE + c) * Y + d) * Z_HI + e,
                            )
                        )
    return out


def swap(value, partner):
    return lax.ppermute(value, ("row", "col"), pairs(partner))


def z_lo_swap(value, d):
    return swap(value, lambda zl, x, q, y, zh: (zl ^ d, x, q, y, zh))


def z_hi_swap(value, first, second):
    return swap(value, lambda zl, x, q, y, zh: (zl, x, q, y, zh ^ (second if q else first)))


def y_swap(value, first, second):
    return swap(value, lambda zl, x, q, y, zh: (zl, x, q, y ^ (second if q else first), zh))


def x_swap(value, first, second):
    return swap(value, lambda zl, x, q, y, zh: (zl, x ^ (second if q else first), q, y, zh))


def core_swap(value):
    return swap(value, lambda zl, x, q, y, zh: (zl, x, q ^ 1, y, zh))


def after(value, *others):
    return lax.optimization_barrier((value, *others))[0]


def hold(value, flops):
    def kernel(in_ref, out_ref):
        out_ref[...] = in_ref[...]

    head = pl.pallas_call(
        kernel,
        out_shape=jax.ShapeDtypeStruct((META, value.shape[1]), value.dtype),
        cost_estimate=pl.CostEstimate(flops=flops, bytes_accessed=0, transcendentals=0),
        name="hold",
    )(value[:META])
    return jnp.concatenate([head, value[META:]])


def pack_kernel(left_index, right_index, left_blocks, right_blocks, left_out, right_out, sems):
    copies = []
    for blocks, out in ((left_blocks, left_out), (right_blocks, right_out)):
        for s in range(blocks.shape[0]):
            copy = pltpu.make_async_copy(
                blocks.at[s], out.at[pl.ds(s * BLK, BLK)], sems.at[len(copies)]
            )
            copy.start()
            copies.append(copy)
    lane = lax.broadcasted_iota(jnp.int32, (META, BLK), 1)

    def write(out, values):
        meta = jnp.zeros((META, BLK), jnp.int32)
        for n, value in enumerate(values):
            meta = jnp.where(lane == n, value, meta)
        out[pl.ds(out.shape[0] - META, META), :] = meta.astype(jnp.float32).astype(jnp.bfloat16)

    row, col = lax.axis_index("row"), lax.axis_index("col")
    columns = [left_index[1, s] for s in range(A_SLOTS)]
    offsets = [jnp.where(k >= 0, k - col * K_COL, -1) for k in columns]
    bands = [jnp.clip(left_index[0, s], 0, 1) for s in range(A_SLOTS)]
    write(left_out, offsets + bands)
    offsets = [right_index[s, 0] - row * K_ROW for s in range(B_SLOTS)]
    live = [o < K_ROW for o in offsets]
    offsets = [jnp.where(f, o, -1) for f, o in zip(live, offsets)]
    write(right_out, offsets + [jnp.where(live[s], right_index[s, 1], 0) for s in range(B_SLOTS)])
    for copy in copies:
        copy.wait()


def pack(left_index, right_index, left_blocks, right_blocks):
    smem = pl.BlockSpec(memory_space=pltpu.SMEM)
    anywhere = pl.BlockSpec(memory_space=pl.ANY)
    vmem = pl.BlockSpec(memory_space=pltpu.VMEM)
    return pl.pallas_call(
        pack_kernel,
        out_shape=[
            jax.ShapeDtypeStruct((A_ROWS, BLK), jnp.bfloat16),
            jax.ShapeDtypeStruct((B_ROWS, BLK), jnp.bfloat16),
        ],
        in_specs=[smem, smem, anywhere, anywhere],
        out_specs=[vmem, vmem],
        scratch_shapes=[pltpu.SemaphoreType.DMA((A_SLOTS + B_SLOTS,))],
        compiler_params=pltpu.CompilerParams(vmem_limit_bytes=56 * 1024 * 1024),
        name="pack",
    )(left_index, right_index, left_blocks, right_blocks)


def gather(left, right):
    rows = A_ROWS
    cat = jnp.concatenate
    sibling = core_swap(left)
    right = cat([right, z_lo_swap(right, 4)])
    z_one = z_hi_swap(cat([left, sibling]), 1, 3)
    right = cat([right, z_lo_swap(right, 2)])
    z_one_mine = hold(z_one[:rows], HOLD)
    right = cat([right, z_lo_swap(right, 1)])
    high = right.shape[0]
    z_two = z_hi_swap(z_one[:rows], 3, 1)
    swapped = core_swap(cat([right, z_one_mine, z_one[rows:]]))
    near_right, z_other = swapped[:high], swapped[high:]
    x_one = x_swap(cat([right, near_right]), 1, 3)
    mine = cat([left, z_one_mine, z_other[rows:]])
    others = cat([sibling, z_one[rows:], z_other[:rows]])
    others, z_two = lax.optimization_barrier((others, z_two))
    y_one = y_swap(cat([mine, others]), 1, 3)
    z_near = y_swap(z_two, 1, 3)
    y_one, z_near = lax.optimization_barrier((y_one, z_near))
    x_two = x_swap(x_one[:high], 3, 1)
    x_other = core_swap(x_one)
    y_two = y_swap(cat([y_one[: 3 * rows], z_two, z_near]), 3, 1)
    swapped = core_swap(cat([x_two, y_one[3 * rows :]]))
    return (
        [mine, y_one[: 3 * rows], y_two, swapped[high:], z_two, z_near],
        [right, near_right, x_one, x_other, x_two, swapped[:high]],
    )


def product_kernel(n_left, n_right, pattern_ref, *refs):
    left_parts = refs[:n_left]
    right_parts = refs[n_left : n_left + n_right]
    out_ref = refs[n_left + n_right]
    (
        left,
        right,
        total,
        left_raw,
        right_raw,
        left_meta,
        right_meta,
        left_keys,
        right_keys,
        work,
        sems,
        raw_sems,
        key_sems,
    ) = refs[n_left + n_right + 1 :]
    raw_copies, copies = [], []
    for parts, raw, rows in ((left_parts, left_raw, A_ROWS), (right_parts, right_raw, B_ROWS)):
        at = 0
        for part in parts:
            n = part.shape[0]
            copy = pltpu.make_async_copy(
                part.at[:, pl.ds(rows - META, META), :],
                raw.at[pl.ds(at, n)],
                raw_sems.at[len(raw_copies)],
            )
            copy.start()
            raw_copies.append(copy)
            at += n
    for parts, held in ((left_parts, left), (right_parts, right)):
        at = 0
        for part in parts:
            n = part.shape[0]
            copy = pltpu.make_async_copy(part, held.at[pl.ds(at, n)], sems.at[len(copies)])
            copy.start()
            copies.append(copy)
            at += n
    total[...] = jnp.zeros_like(total)
    for copy in raw_copies:
        copy.wait()
    n_a, n_b = left_meta.shape[0], right_meta.shape[0]
    for i in range(n_a):
        left_meta[pl.ds(i, 1), :] = left_raw[i].astype(jnp.float32)[0:1].astype(jnp.int32)
    for i in range(n_b):
        right_meta[pl.ds(i, 1), :] = right_raw[i].astype(jnp.float32)[0:1].astype(jnp.int32)
    right_copy = pltpu.make_async_copy(right_meta, right_keys, key_sems.at[1])
    right_copy.start()

    row, col = lax.axis_index("row"), lax.axis_index("col")
    zl, x, q = row // (X * CORE), (row // CORE) % X, row % CORE
    y, zh = col // Z_HI, col % Z_HI
    near, far = jnp.where(q == 0, 1, 3), jnp.where(q == 0, 3, 1)
    i = lax.broadcasted_iota(jnp.int32, left_meta.shape, 0)
    lane = lax.broadcasted_iota(jnp.int32, left_meta.shape, 1)
    first = i < 9
    n = jnp.where(first, i, i - 2)
    r = (n >= 3).astype(jnp.int32) + (n >= 6).astype(jnp.int32) + (n >= 9).astype(jnp.int32)
    p = n - 3 * r
    one = jnp.where(first, near, far)
    two = jnp.where(first, far, near)
    dz = jnp.where(p == 0, 0, jnp.where(p == 1, one, two))
    dy = jnp.where(r == 0, 0, jnp.where(r == 1, near, jnp.where(r == 2, 2, far)))
    opposite = (i == 9) | (i == 10) | (i > 13)
    dz = jnp.where(opposite, 2, dz)
    dy = jnp.where(
        opposite,
        jnp.where(i == 9, far, jnp.where(i == 10, 2, jnp.where(i == 14, 0, near))),
        dy,
    )
    there = ((y ^ dy) << 2) + (zh ^ dz)
    meta = left_meta[...]
    live = meta >= 0
    offset = jnp.maximum(meta, 0)
    group = jnp.zeros_like(offset)
    for bound in range(K_ROW, K_COL, K_ROW):
        group += (offset >= bound).astype(jnp.int32)
    want = jnp.where(live, offset - group * K_ROW, K_ROW)
    other = there * (K_COL // K_ROW) + group
    e = (other & 1) ^ q
    u = ((other >> 1) & 3) ^ x
    w = (other >> 3) ^ zl
    m = ((w & 1) << 2) | (w & 2) | (w >> 2)
    part = jnp.where(
        u == 0,
        e,
        jnp.where(u == 2, 6 + e, jnp.where(u == near, 2 + e, 5 - e)),
    )
    code = ((part * Z_LO + m) << 8) | want
    left_meta[...] = jnp.where(lane < A_SLOTS, code, meta)
    left_copy = pltpu.make_async_copy(left_meta, left_keys, key_sems.at[0])
    left_copy.start()
    right_copy.wait()
    left_copy.wait()
    slab = pattern_ref.shape[1]
    spare = pattern_ref.shape[0] * slab

    def shard(i, count):
        for s in range(A_SLOTS):
            found = left_keys[i, s]
            band = left_keys[i, A_SLOTS + s]
            t = found >> 8
            wanted = found & 255
            for j in range(B_SLOTS):
                column = right_keys[t, B_SLOTS + j]
                hit = (right_keys[t, j] == wanted) & (pattern_ref[band, column] > 0)
                work[0, count] = i * A_SLOTS + s
                work[1, count] = t * B_SLOTS + j
                work[2, count] = band * slab + column
                count = count + hit.astype(jnp.int32)
        return count

    count = lax.fori_loop(0, n_a, shard, jnp.int32(0))
    for n in range(GROUP):
        work[0, count + n] = 0
        work[1, count + n] = 0
        work[2, count + n] = spare
    for copy in copies:
        copy.wait()

    def multiply(g, carry):
        products = []
        for n in range(GROUP):
            a, b = work[0, g * GROUP + n], work[1, g * GROUP + n]
            a_shard = a // A_SLOTS
            a_at = pl.multiple_of((a - a_shard * A_SLOTS) * BLK, BLK)
            b_at = pl.multiple_of((b & 1) * BLK, BLK)
            products.append(
                jnp.dot(
                    left[a_shard, pl.ds(a_at, BLK), :],
                    right[b >> 1, pl.ds(b_at, BLK), :],
                    preferred_element_type=jnp.float32,
                )
            )
        for n in range(GROUP):
            total[work[2, g * GROUP + n]] += products[n]
        return carry

    lax.fori_loop(0, (count + GROUP - 1) // GROUP, multiply, 0)
    for b in range(pattern_ref.shape[0]):
        for j in range(slab):
            out_ref[b * BLK : (b + 1) * BLK, j * BLK : (j + 1) * BLK] = total[b * slab + j].astype(
                out_ref.dtype
            )


def multiply_parts(left_parts, right_parts, pattern):
    band, slab = pattern.shape
    left_parts = [p.reshape(-1, A_ROWS, BLK) for p in left_parts]
    right_parts = [p.reshape(-1, B_ROWS, BLK) for p in right_parts]
    n_a = sum(p.shape[0] for p in left_parts)
    n_b = sum(p.shape[0] for p in right_parts)
    n_parts = len(left_parts) + len(right_parts)
    smem = pl.BlockSpec(memory_space=pltpu.SMEM)
    anywhere = pl.BlockSpec(memory_space=pl.ANY)

    def kernel(*refs):
        product_kernel(len(left_parts), len(right_parts), *refs)

    return pl.pallas_call(
        kernel,
        out_shape=jax.ShapeDtypeStruct((band * BLK, slab * BLK), jnp.bfloat16),
        in_specs=[smem] + [anywhere] * n_parts,
        out_specs=pl.BlockSpec(memory_space=pltpu.VMEM),
        scratch_shapes=[
            pltpu.VMEM((n_a, A_ROWS, BLK), jnp.bfloat16),
            pltpu.VMEM((n_b, B_ROWS, BLK), jnp.bfloat16),
            pltpu.VMEM((band * slab + 1, BLK, BLK), jnp.float32),
            pltpu.VMEM((n_a, META, BLK), jnp.bfloat16),
            pltpu.VMEM((n_b, META, BLK), jnp.bfloat16),
            pltpu.VMEM((n_a, BLK), jnp.int32),
            pltpu.VMEM((n_b, BLK), jnp.int32),
            pltpu.SMEM((n_a, BLK), jnp.int32),
            pltpu.SMEM((n_b, BLK), jnp.int32),
            pltpu.SMEM((3, n_a * A_SLOTS * B_SLOTS + GROUP), jnp.int32),
            pltpu.SemaphoreType.DMA((n_parts,)),
            pltpu.SemaphoreType.DMA((n_parts,)),
            pltpu.SemaphoreType.DMA((2,)),
        ],
        compiler_params=pltpu.CompilerParams(vmem_limit_bytes=24 * 1024 * 1024),
        name="block_products",
    )(pattern, *left_parts, *right_parts)


def per_device(left_blocks, left_index, right_blocks, right_index, out_pattern):
    left, right = pack(left_index.T, right_index, left_blocks, right_blocks)
    return multiply_parts(*gather(left, right), out_pattern)


def solution(mesh):
    placed = (
        P("row", "col", None),
        P("row", "col"),
        P("row", "col", None),
        P("row", "col"),
        P("row", "col"),
    )
    return jax.shard_map(
        per_device, mesh=mesh, in_specs=placed, out_specs=P("row", "col"), check_vma=False
    )
```
